512 devices in a mesh: rep: 8 (over y), head: 64 (over z, x, core).
Axes of the slice: x: 4, y: 8, z: 8, core: 2. Of those that a mesh axis runs over, the one named last changes fastest.
Arguments:
- query: bfloat16 [8, 8192, 8192], P('rep', 'head'), may hold values from -16 to 16
- key: bfloat16 [8, 8192, 1024], P('rep', 'head'), may hold values from -16 to 16
- value: bfloat16 [8, 8192, 1024], P('rep', 'head'), may hold values from -6 to 6
- lengths: int32 [8, 8], P('rep'), may hold values from 1 to 4096, 8192 in all within a row
Outputs:
- attended: bfloat16 [8, 8192, 8192], P('rep', 'head')
The draws below stay inside these ranges and needn't reach their ends.
Inputs may be any that keep to these rules, and one draw needn't show every extreme that they name: Each slab's 8 lengths sum to 8192, and the longest is exactly 4096.
All inputs are finite; a program needn't handle non-finite values.
Results may differ from the reference program's by a relative error of at most 0.0038.
Values may be sent and summed in bfloat16 or wider, within the bound.
A program may use at most 64 MiB of HBM per device.

```python
import math
import jax
import jax.numpy as jnp
import numpy as np
from jax import lax

Q_HEADS = 64
KV_HEADS = 8
HEAD_DIM = 128
DOCS = 8
REPLICAS = 8
SLAB = 8192
MAXDOC = 4096


def shared_rows(key):
    return jax.random.normal(jax.random.fold_in(key, 11), (REPLICAS, SLAB, KV_HEADS * HEAD_DIM), jnp.float32)


def draw_key(key, part):
    base = shared_rows(key)
    return jnp.clip(base, -6.0, 6.0).astype(jnp.bfloat16)


def draw_query(key, part):
    key = jax.random.fold_in(key, 5)
    fresh = jax.random.normal(key, (REPLICAS, SLAB, Q_HEADS * HEAD_DIM), jnp.float32)
    return jnp.clip(fresh, -6.0, 6.0).astype(jnp.bfloat16)


def levels(key, shape, split, smallest, high):
    level, own = 1.0, jax.random.fold_in(key, 6)
    for dim, parts in split:
        steps = jnp.exp(jax.random.uniform(jax.random.fold_in(own, dim), (parts,), jnp.float32, smallest / len(split), high / len(split)))
        level = level * jnp.repeat(steps, shape[dim] // parts).reshape([-1 if axis == dim else 1 for axis in range(len(shape))])
    return level


def split_up(amount, total, most, slope):
    weights = [(1 << 20) // math.isqrt(standing ** slope) + 1 for standing in range(2, amount + 1)]
    rest, holding = total - most - (amount - 1), [1] * (amount - 1)
    while rest > 0:
        candidates = [i for i in range(amount - 1) if holding[i] < most]
        pool, left = sum([weights[i] for i in candidates]), rest
        for i in candidates:
            more = min(most - holding[i], max(1, left * weights[i] // pool), rest)
            holding[i] = holding[i] + more
            rest = rest - more
    return np.array([most] + holding)


def ragged(key, amount, total, reach, skew):
    if amount == 2:
        one = jax.random.randint(key, (), max(1, total - reach), min(reach, total - 1) + 1)
        return jnp.stack([one, total - one])
    sizes = jnp.asarray(split_up(amount, total, reach, skew), jnp.int32)
    couples = (amount - 1) // 2
    source_of, receiver = sizes[1:1 + 2 * couples:2], sizes[2:2 + 2 * couples:2]
    room = jnp.minimum(source_of - 1, reach - receiver)
    passed = jax.random.randint(jax.random.fold_in(key, 1), (couples,), 0, 1 << 20) % (room + 1)
    sizes = sizes.at[1:1 + 2 * couples:2].set(source_of - passed).at[2:2 + 2 * couples:2].set(receiver + passed)
    return sizes[jax.random.permutation(jax.random.fold_in(key, 2), amount)]


def centred(stream_key, dims, deviation, most, pieces=(), kind=jnp.bfloat16):
    values = deviation * jax.random.normal(stream_key, dims, jnp.float32)
    if pieces:
        values = values * levels(stream_key, dims, pieces, -0.22, 0.18)
    return jnp.clip(values, -most, most).astype(kind)


def setup_inputs(seed: int = 0) -> dict:
    seeds = jax.random.split(jax.random.key(seed), 5)
    return {
        "query": draw_query(jax.random.fold_in(seeds[4], 71), 0),
        "key": draw_key(jax.random.fold_in(seeds[4], 71), 0),
        "value": centred(seeds[2], (REPLICAS, SLAB, KV_HEADS * HEAD_DIM), 1.0, 6.0, ((0, 8), (1, 64))),
        "lengths": jax.vmap(lambda own: ragged(own, DOCS, SLAB, MAXDOC, 2))(jax.random.split(seeds[3], REPLICAS)).reshape((REPLICAS, DOCS)).astype(jnp.int32),
    }


def doc_starts(doc_lengths, count):
    ends = jnp.cumsum(doc_lengths)
    places = jnp.arange(count, dtype=jnp.int32)
    picked = jnp.where(ends[None, :] <= places[:, None], doc_lengths[None, :], 0)
    return jnp.sum(picked, axis=1).astype(jnp.int32)


def attend_tile(queries, keys, values, starts, index, tile):
    heads = queries.shape[1]
    q_block = lax.dynamic_slice_in_dim(queries, index * tile, tile, 0).astype(jnp.float32)
    q_pos = index * tile + jnp.arange(tile, dtype=jnp.int32)
    q_start = lax.dynamic_slice_in_dim(starts, index * tile, tile, 0)
    first = (q_start[0] // tile).astype(jnp.int32)
    scale = float(HEAD_DIM) ** -0.5

    def visit(block, carry):
        top, total, accum = carry
        k_block = lax.dynamic_slice_in_dim(keys, block * tile, tile, 0).astype(jnp.float32)
        v_block = lax.dynamic_slice_in_dim(values, block * tile, tile, 0).astype(jnp.float32)
        scores = jnp.einsum("qhd,khd->hqk", q_block, k_block) * scale
        k_pos = block * tile + jnp.arange(tile, dtype=jnp.int32)
        allowed = (k_pos[None, :] <= q_pos[:, None]) & (k_pos[None, :] >= q_start[:, None])
        scores = jnp.where(allowed[None], scores, jnp.float32(-1e30))
        new_top = jnp.maximum(top, jnp.max(scores, axis=2))
        weights = jnp.where(allowed[None], jnp.exp(scores - new_top[:, :, None]), jnp.float32(0.0))
        factor = jnp.exp(top - new_top)
        rounded = weights.astype(jnp.bfloat16).astype(jnp.float32)
        accum = accum * factor[:, :, None] + jnp.einsum("hqk,khd->hqd", rounded, v_block)
        total = total * factor + jnp.sum(weights, axis=2)
        return new_top, total, accum

    start_state = (jnp.full((heads, tile), -1e30, jnp.float32), jnp.zeros((heads, tile), jnp.float32),
                   jnp.zeros((heads, tile, HEAD_DIM), jnp.float32))
    top, total, accum = lax.fori_loop(first, (index + 1).astype(jnp.int32), visit, start_state)
    result = (accum / total[:, :, None]).astype(jnp.bfloat16)
    return jnp.transpose(result, (1, 0, 2))


def one_slab(inputs):
    queries, keys, values, doc_lengths = inputs
    count = queries.shape[0]
    tile = min(512, count)
    starts = doc_starts(doc_lengths, count)
    queries = queries.reshape(count, Q_HEADS, HEAD_DIM)
    group = Q_HEADS // KV_HEADS
    keys = jnp.repeat(keys.reshape(count, KV_HEADS, HEAD_DIM), group, axis=1)
    values = jnp.repeat(values.reshape(count, KV_HEADS, HEAD_DIM), group, axis=1)

    def per_tile(index):
        return attend_tile(queries, keys, values, starts, index, tile)

    blocks = lax.map(per_tile, jnp.arange(count // tile, dtype=jnp.int32))
    return blocks.reshape(count, Q_HEADS * HEAD_DIM)


def reference(query, key, value, lengths):
    return lax.map(one_slab, (query, key, value, lengths))
```

```python
import functools

import jax
import jax.numpy as jnp
from jax import lax
from jax.experimental import pallas as pl
from jax.experimental.pallas import tpu as pltpu
from jax.sharding import PartitionSpec as P

MESH = pl.DeviceIdType.MESH
F32 = jnp.float32
BF16 = jnp.bfloat16

HEADS = 8
DIM = 128
DOCS = 8
GROUP = 8
TOK = 128
SLICE = GROUP * TOK
WINDOW = 4
QB = 512
LOG2E_SCALE = 1.4426950408889634 * DIM**-0.5
OFF = -1e30


def kernel(slices, lengths, q_in, k_in, v_in, out, qb, kb, vt, v_raw, v_turned, q_doc, k_doc,
           top, total, accum, held, held_top, done,
           q_send, q_recv, kv_send, kv_recv, ring_send, ring_recv, out_send, out_recv, local_sem):
    rep = lax.axis_index("rep")
    me = lax.axis_index("head")
    z, g = me // GROUP, me % GROUP

    def peer(t):
        return (g + t) % GROUP

    def source(t):
        return (g - t + GROUP) % GROUP

    def device(zz, gg):
        return (rep, zz * GROUP + gg)

    def block(i, size=TOK):
        return pl.ds(pl.multiple_of(i * size, size), size)

    barrier = pltpu.get_barrier_semaphore()
    for t in range(1, GROUP):
        pl.semaphore_signal(barrier, inc=1, device_id=device(z, peer(t)), device_id_type=MESH)
    for step in (1, slices - 1):
        pl.semaphore_signal(barrier, inc=1, device_id=device((z + step) % slices, g), device_id_type=MESH)
    v_load = pltpu.make_async_copy(v_in, v_raw, local_sem.at[0])
    v_load.start()
    pl.semaphore_wait(barrier, GROUP + 1)

    def k_copy(t, to, row):
        src, dst = k_in.at[:, block(to)], kb.at[0, block(row), :]
        if t == 0:
            return pltpu.make_async_copy(src, dst, local_sem.at[1])
        return pltpu.make_async_remote_copy(src, dst, kv_send.at[0, t], kv_recv.at[0, t], device_id=device(z, to), device_id_type=MESH)

    def v_copy(t, to, row):
        src, dst = v_turned.at[to], vt.at[0, :, block(row)]
        if t == 0:
            return pltpu.make_async_copy(src, dst, local_sem.at[2])
        return pltpu.make_async_remote_copy(src, dst, kv_send.at[1, t], kv_recv.at[1, t], device_id=device(z, to), device_id_type=MESH)

    def q_copy(h, t, to, row):
        src, dst = q_in.at[:, block(to * HEADS + h)], qb.at[h, block(row), :]
        if t == 0:
            return pltpu.make_async_copy(src, dst, q_recv.at[h, 0])
        return pltpu.make_async_remote_copy(src, dst, q_send.at[h, t], q_recv.at[h, t], device_id=device(z, to), device_id_type=MESH)

    def out_copy(h, t, to, head_group):
        src, dst = done.at[h, block(to), :], out.at[:, block(head_group * HEADS + h)]
        if t == 0:
            return pltpu.make_async_copy(src, dst, out_recv.at[h, 0])
        return pltpu.make_async_remote_copy(src, dst, out_send.at[h, t], out_recv.at[h, t], device_id=device(z, to), device_id_type=MESH)

    def ring_copies(s):
        to = device((z + 1) % slices, g)
        return [
            pltpu.make_async_remote_copy(kb.at[s], kb.at[s + 1], ring_send.at[s, 0], ring_recv.at[s, 0], device_id=to, device_id_type=MESH),
            pltpu.make_async_remote_copy(vt.at[s], vt.at[s + 1], ring_send.at[s, 1], ring_recv.at[s, 1], device_id=to, device_id_type=MESH),
        ]

    for t in range(GROUP):
        k_copy(t, peer(t), g).start()
    v_load.wait()
    for i in range(GROUP):
        v_turned[i] = v_raw[:, i * TOK:(i + 1) * TOK].astype(F32).T.astype(BF16)
    for t in range(GROUP):
        v_copy(t, peer(t), g).start()

    def send_queries(h, _):
        for t in range(GROUP):
            q_copy(h, t, peer(t), g).start()
        return 0

    lax.fori_loop(0, HEADS, send_queries, 0)

    lane = lax.broadcasted_iota(jnp.int32, (1, DIM), 1)
    first = jnp.zeros((1, DIM), jnp.int32)
    last = jnp.zeros((1, DIM), jnp.int32)
    end = jnp.int32(0)
    for d in range(DOCS):
        begin = end
        end = end + lengths[0, d]
        first = jnp.where(lane == d, begin, first)
        last = jnp.where(lane == d, end, last)
    row = lax.broadcasted_iota(jnp.int32, (SLICE, DIM), 0)

    def within(base):
        spot = row + base
        return (spot >= first) & (spot < last)

    q_doc[...] = jnp.where(within(z * SLICE) | (lane >= DOCS), jnp.float32(0), jnp.float32(OFF)).astype(BF16)

    def fill(s, _):
        k_doc[s] = jnp.where(within((z - s) * SLICE), jnp.float32(1), jnp.float32(0)).astype(BF16)
        return 0

    lax.fori_loop(0, WINDOW + 1, fill, 0)

    def scores(h, step):
        b, s, lo, hi, diagonal = step
        query = jnp.concatenate([qb[h, b * QB:(b + 1) * QB, :], q_doc[b * QB:(b + 1) * QB, :]], axis=1)
        keys = jnp.concatenate([kb[s, lo:hi, :], k_doc[s, lo:hi, :]], axis=1)
        found = lax.dot_general(keys, query, (((1,), (1,)), ((), ())), preferred_element_type=F32)
        if diagonal:
            k_pos = lax.broadcasted_iota(jnp.int32, found.shape, 0) + lo
            q_pos = lax.broadcasted_iota(jnp.int32, found.shape, 1) + b * QB
            found = jnp.where(k_pos <= q_pos, found, jnp.float32(OFF))
        return found, jnp.max(found, axis=0, keepdims=True)

    def unit(h, steps, fresh=False, following=None):
        state = {}
        now = (held[...], held_top[...]) if following is not None else scores(h, steps[0])
        for i, (b, s, lo, hi, _) in enumerate(steps):
            cols = slice(b * QB, (b + 1) * QB)
            later = None
            if i + 1 < len(steps):
                later = scores(h, steps[i + 1])
            elif following is not None:
                held[...], held_top[...] = scores(following, steps[0])
            found, best = now
            if b not in state and not fresh:
                state[b] = (top[h, :, cols], total[h, :, cols], accum[h, :, cols])
            if b in state:
                old, norm, acc = state[b]
                best = jnp.maximum(old, best)
            weights = jnp.exp2((found - best) * LOG2E_SCALE)
            product = jnp.dot(vt[s, :, lo:hi], weights.astype(BF16), preferred_element_type=F32)
            added = jnp.sum(weights, axis=0, keepdims=True)
            if b in state:
                factor = jnp.exp2((old - best) * LOG2E_SCALE)
                state[b] = (best, norm * factor + added, acc * factor + product)
            else:
                state[b] = (best, added, product)
            if not any(other[0] == b for other in steps[i + 1:]):
                top[h, :, cols], total[h, :, cols], accum[h, :, cols] = state[b]
            now = later

    blocks = SLICE // QB
    diag = [(b, 0, 0, (b + 1) * QB, True) for b in range(blocks)]
    far = [(b, WINDOW, b * QB, SLICE, False) for b in range(blocks)]

    def full(s):
        return [(b, s, 0, SLICE, False) for b in range(blocks)]

    def sweep(lo, hi, steps, before=None, after=None):
        held[...], held_top[...] = scores(lo, steps[0])

        def body(h, _):
            if before is not None:
                before(h)
            unit(h, steps, following=jnp.minimum(h + 1, hi - 1))
            if after is not None:
                after(h)
            return 0

        lax.fori_loop(lo, hi, body, 0)

    def wait_queries(h):
        for t in range(GROUP):
            copy = q_copy(h, t, g, source(t))
            copy.wait() if t == 0 else copy.wait_recv()

    def arrive(s):
        @pl.when(z >= s)
        def _():
            for copy in ring_copies(s - 1):
                copy.wait_recv()

    def pass_on(s):
        @pl.when((z >= s) & (z < slices - 1))
        def _():
            for copy in ring_copies(s):
                copy.start()

    def finish(h):
        for b in range(blocks):
            cols = slice(b * QB, (b + 1) * QB)
            done[h, cols, :] = (accum[h, :, cols] / total[h, :, cols]).T.astype(BF16)
        for t in range(GROUP):
            out_copy(h, t, peer(t), g).start()

    for t in range(GROUP):
        copy = k_copy(t, g, source(t))
        copy.wait() if t == 0 else copy.wait_recv()
    for t in range(GROUP):
        copy = v_copy(t, g, source(t))
        copy.wait() if t == 0 else copy.wait_recv()
    pass_on(0)

    half = HEADS // 2

    def opening(h, _):
        wait_queries(h)
        unit(h, diag, fresh=True)
        return 0

    lax.fori_loop(0, half, opening, 0)
    arrive(1)
    pass_on(1)

    @pl.when(z >= 1)
    def _():
        sweep(0, half, full(1))

    def middle(h, _):
        wait_queries(h)

        @pl.when(h == half + 2)
        def _():
            arrive(2)
            pass_on(2)

        @pl.when(z >= 1)
        def _():
            unit(h, diag + full(1), fresh=True)

        @pl.when(z < 1)
        def _():
            unit(h, diag, fresh=True)

        return 0

    lax.fori_loop(half, HEADS, middle, 0)

    def relay(h):
        @pl.when(h == half)
        def _():
            arrive(3)
            pass_on(3)

    @pl.when(z >= 2)
    def _():
        sweep(0, HEADS, full(2), before=relay)

    def last_wait(h):
        @pl.when(h == 0)
        def _():
            arrive(4)

    @pl.when(z >= 4)
    def _():
        sweep(0, HEADS, full(3) + far, before=last_wait, after=finish)

    @pl.when(z == 3)
    def _():
        sweep(0, HEADS, full(3), after=finish)

    @pl.when(z < 3)
    def _():
        def body(h, _):
            finish(h)
            return 0

        lax.fori_loop(0, HEADS, body, 0)

    for t in range(1, GROUP):
        k_copy(t, peer(t), g).wait_send()
        v_copy(t, peer(t), g).wait_send()
    for s in range(WINDOW):
        @pl.when((z >= s) & (z < slices - 1))
        def _():
            for copy in ring_copies(s):
                copy.wait_send()

    def closing(h, _):
        for t in range(1, GROUP):
            q_copy(h, t, peer(t), g).wait_send()
            out_copy(h, t, peer(t), g).wait_send()
        for t in range(GROUP):
            copy = out_copy(h, t, g, source(t))
            copy.wait() if t == 0 else copy.wait_recv()
        return 0

    lax.fori_loop(0, HEADS, closing, 0)


def solution(mesh):
    slices = mesh.shape["head"] // GROUP

    def local(query, key, value, lengths):
        rows, width = query.shape[1:]
        hbm = pl.BlockSpec(memory_space=pl.ANY)
        dma = pltpu.SemaphoreType.DMA
        attended = pl.pallas_call(
            functools.partial(kernel, slices),
            out_shape=jax.ShapeDtypeStruct((rows, width), BF16),
            in_specs=[pl.BlockSpec(memory_space=pltpu.SMEM), hbm, hbm, hbm],
            out_specs=hbm,
            scratch_shapes=[
                pltpu.VMEM((HEADS, SLICE, DIM), BF16),
                pltpu.VMEM((WINDOW + 1, SLICE, DIM), BF16),
                pltpu.VMEM((WINDOW + 1, DIM, SLICE), BF16),
                pltpu.VMEM((TOK, GROUP * DIM), BF16),
                pltpu.VMEM((GROUP, DIM, TOK), BF16),
                pltpu.VMEM((SLICE, DIM), BF16),
                pltpu.VMEM((WINDOW + 1, SLICE, DIM), BF16),
                pltpu.VMEM((HEADS, 1, SLICE), F32),
                pltpu.VMEM((HEADS, 1, SLICE), F32),
                pltpu.VMEM((HEADS, DIM, SLICE), F32),
                pltpu.VMEM((SLICE, QB), F32),
                pltpu.VMEM((1, QB), F32),
                pltpu.VMEM((HEADS, SLICE, DIM), BF16),
                dma((HEADS, GROUP)),
                dma((HEADS, GROUP)),
                dma((2, GROUP)),
                dma((2, GROUP)),
                dma((WINDOW, 2)),
                dma((WINDOW, 2)),
                dma((HEADS, GROUP)),
                dma((HEADS, GROUP)),
                dma((3,)),
            ],
            compiler_params=pltpu.CompilerParams(collective_id=0, has_side_effects=True, vmem_limit_bytes=56 * 2**20),
        )(lengths, query[0], key[0], value[0])
        return attended[None]

    placed = (P("rep", "head", None), P("rep", "head", None), P("rep", "head", None), P("rep", None))
    return jax.shard_map(local, mesh=mesh, in_specs=placed, out_specs=P("rep", "head", None), check_vma=False)
```

```python
import functools

import jax
import jax.numpy as jnp
from jax import lax
from jax.experimental import pallas as pl
from jax.experimental.pallas import tpu as pltpu
from jax.sharding import PartitionSpec as P

MESH = pl.DeviceIdType.MESH
F32 = jnp.float32
BF16 = jnp.bfloat16

HEADS = 8
DIM = 128
DOCS = 8
GROUP = 8
TOK = 128
SLICE = GROUP * TOK
HALF = SLICE // 2
WINDOW = 4
QB = 512
LOG2E_SCALE = 1.4426950408889634 * DIM**-0.5
OFF = -1e30


def kernel(slices, lengths, q_in, k_in, v_in, out, qb, kb, vt, v_raw, v_turned, q_doc, k_doc,
           top, total, accum, held, held_top, done,
           k_relay, v_relay,
           q_send, q_recv, kv_send, kv_recv, ring_send, ring_recv, back_send, back_recv, out_send, out_recv, local_sem, ready):
    rep = lax.axis_index("rep")
    me = lax.axis_index("head")
    z, g = me // GROUP, me % GROUP

    def peer(t):
        return (g + t) % GROUP

    def device(zz, gg):
        return (rep, zz * GROUP + gg)

    def block(i, size=TOK):
        return pl.ds(pl.multiple_of(i * size, size), size)

    def when(condition, action):
        pl.when(condition)(action)

    barrier = pltpu.get_barrier_semaphore()

    def greet(zz):
        pl.semaphore_signal(barrier, inc=1, device_id=device(zz, g), device_id_type=MESH)

    def answer(i, zz):
        pl.semaphore_signal(ready.at[i], inc=1, device_id=device(zz, g), device_id_type=MESH)

    v_load = pltpu.make_async_copy(v_in, v_raw, local_sem.at[0])
    v_load.start()
    for t in range(1, GROUP):
        pl.semaphore_signal(barrier, inc=1, device_id=device(z, peer(t)), device_id_type=MESH)
    when(z < slices - 1, lambda: greet(z + 1))
    when(z == 0, lambda: greet(slices - 1))
    when(z == WINDOW, lambda: greet(slices - 1))
    when(z < slices - 1 - WINDOW, lambda: greet(z + 1 + WINDOW))
    expected = jnp.where(z > 0, GROUP, GROUP - 1) + jnp.where(z > WINDOW, 1, 0) + jnp.where(z == slices - 1, 2, 0)
    pl.semaphore_wait(barrier, expected)
    when(z > 0, lambda: answer(0, z - 1))
    when(z == slices - 1, lambda: answer(1, 0))
    when(z > WINDOW, lambda: answer(2, z - 1 - WINDOW))

    def copy_to(t, src, dst, send, recv):
        if t == 0:
            return pltpu.make_async_copy(src, dst, recv)
        return pltpu.make_async_remote_copy(src, dst, send, recv, device_id=device(z, peer(t)), device_id_type=MESH)

    def k_copy(t):
        return copy_to(t, k_in.at[:, block(peer(t))], kb.at[0, block(g), :], kv_send.at[0], kv_recv.at[0])

    def v_copy(t):
        return copy_to(t, v_turned.at[peer(t)], vt.at[0, :, block(g)], kv_send.at[1], kv_recv.at[1])

    def q_copy(h, t):
        return copy_to(t, q_in.at[:, block(peer(t) * HEADS + h)], qb.at[h, block(g), :], q_send.at[0], q_recv.at[h])

    def out_copy(h, t):
        return copy_to(t, done.at[h, block(peer(t)), :], out.at[:, block(g * HEADS + h)], out_send.at[0], out_recv.at[0])

    def wait_bytes(ref, sem):
        pltpu.make_async_copy(ref, ref, sem).wait()

    def half_refs(s, j):
        part = pl.ds(j * HALF, HALF)
        return kb.at[s, part, :], vt.at[s, :, part]

    def remote(pairs, send, recv, to):
        return [pltpu.make_async_remote_copy(src, dst, send, recv, device_id=device(to, g), device_id_type=MESH) for src, dst in pairs]

    def ring_copies(s, j):
        return remote(zip(half_refs(s, j), half_refs(s + 1, j)), ring_send.at[s, j], ring_recv.at[s, j], (z + 1) % slices)

    def back_copies(hop):
        if hop == 0:
            return remote(zip(half_refs(0, 0), (k_relay, v_relay)), back_send.at[0], back_recv.at[0], (z + slices - 1) % slices)
        return remote(zip((k_relay, v_relay), half_refs(WINDOW, 0)), back_send.at[1], back_recv.at[1], (z + WINDOW + 1) % slices)

    def wait_half(sem):
        wait_bytes(kb.at[0], sem)

    sends_back = z < slices - WINDOW
    relays = (z < slices - 1 - WINDOW) | (z == slices - 1)

    for t in range(GROUP):
        k_copy(t).start()
    v_load.wait()
    for i in range(GROUP):
        v_turned[i] = v_raw[:, i * TOK:(i + 1) * TOK].astype(F32).T.astype(BF16)
    for t in range(GROUP):
        v_copy(t).start()

    def send_queries(h, _):
        for t in range(GROUP):
            q_copy(h, t).start()
        return 0

    lax.fori_loop(0, HEADS, send_queries, 0)

    lane = lax.broadcasted_iota(jnp.int32, (1, DIM), 1)
    first = jnp.zeros((1, DIM), jnp.int32)
    last = jnp.zeros((1, DIM), jnp.int32)
    end = jnp.int32(0)
    for d in range(DOCS):
        begin = end
        end = end + lengths[0, d]
        first = jnp.where(lane == d, begin, first)
        last = jnp.where(lane == d, end, last)
    row = lax.broadcasted_iota(jnp.int32, (SLICE, DIM), 0)

    def within(base):
        spot = row + base
        return (spot >= first) & (spot < last)

    q_doc[...] = jnp.where(within(z * SLICE) | (lane >= DOCS), jnp.float32(0), jnp.float32(OFF)).astype(BF16)

    def fill(s, _):
        k_doc[s] = jnp.where(within((z - s) * SLICE), jnp.float32(1), jnp.float32(0)).astype(BF16)
        return 0

    lax.fori_loop(0, WINDOW + 1, fill, 0)

    def scores(h, step):
        b, s, lo, hi, diagonal = step
        query = jnp.concatenate([qb[h, b * QB:(b + 1) * QB, :], q_doc[b * QB:(b + 1) * QB, :]], axis=1)
        keys = jnp.concatenate([kb[s, lo:hi, :], k_doc[s, lo:hi, :]], axis=1)
        found = lax.dot_general(keys, query, (((1,), (1,)), ((), ())), preferred_element_type=F32)
        if diagonal:
            k_pos = lax.broadcasted_iota(jnp.int32, found.shape, 0) + lo
            q_pos = lax.broadcasted_iota(jnp.int32, found.shape, 1) + b * QB
            found = jnp.where(k_pos <= q_pos, found, jnp.float32(OFF))
        return found, jnp.max(found, axis=0, keepdims=True)

    def unit(h, steps, fresh=False, following=None):
        state = {}
        now = (held[...], held_top[...]) if following is not None else scores(h, steps[0])
        for i, (b, s, lo, hi, _) in enumerate(steps):
            cols = slice(b * QB, (b + 1) * QB)
            later = None
            if i + 1 < len(steps):
                later = scores(h, steps[i + 1])
            elif following is not None:
                held[...], held_top[...] = scores(following, steps[0])
            found, best = now
            if b not in state and not fresh:
                state[b] = (top[h, :, cols], total[h, :, cols], accum[h, :, cols])
            if b in state:
                old, norm, acc = state[b]
                best = jnp.maximum(old, best)
            weights = jnp.exp2((found - best) * LOG2E_SCALE)
            product = jnp.dot(vt[s, :, lo:hi], weights.astype(BF16), preferred_element_type=F32)
            added = jnp.sum(weights, axis=0, keepdims=True)
            if b in state:
                factor = jnp.exp2((old - best) * LOG2E_SCALE)
                state[b] = (best, norm * factor + added, acc * factor + product)
            else:
                state[b] = (best, added, product)
            if not any(other[0] == b for other in steps[i + 1:]):
                top[h, :, cols], total[h, :, cols], accum[h, :, cols] = state[b]
            now = later

    blocks = SLICE // QB
    diag = [(b, 0, 0, (b + 1) * QB, True) for b in range(blocks)]
    far = [(b, WINDOW, b * QB, SLICE, False) for b in range(blocks)]

    def full(s):
        return [(b, s, 0, SLICE, False) for b in range(blocks)]

    def sweep(lo, hi, steps, before=None, after=None):
        held[...], held_top[...] = scores(lo, steps[0])

        def body(h, _):
            if before is not None:
                before(h)
            unit(h, steps, following=jnp.minimum(h + 1, hi - 1))
            if after is not None:
                after(h)
            return 0

        lax.fori_loop(lo, hi, body, 0)

    def wait_queries(h):
        wait_bytes(qb.at[h], q_recv.at[h])

    def start(copies):
        def act():
            for copy in copies:
                copy.start()
        return act

    def arrive(s, j):
        when(z >= s, lambda: wait_half(ring_recv.at[s - 1, j]))

    def pass_on(s, j):
        when((z >= s) & (z < slices - 1), start(ring_copies(s, j)))

    def relay_back():
        when(z < slices - 1 - WINDOW, lambda: pl.semaphore_wait(ready.at[2], 1))
        when(relays, lambda: wait_half(back_recv.at[0]))
        when(relays, start(back_copies(1)))

    def finish(h):
        for b in range(blocks):
            cols = slice(b * QB, (b + 1) * QB)
            done[h, cols, :] = (accum[h, :, cols] / total[h, :, cols]).T.astype(BF16)
        for t in range(GROUP):
            out_copy(h, t).start()

    wait_bytes(kb.at[0], kv_recv.at[0])
    wait_bytes(vt.at[0], kv_recv.at[1])
    when(z < slices - 1, lambda: pl.semaphore_wait(ready.at[0], 1))
    pass_on(0, 1)
    when(z == 0, lambda: pl.semaphore_wait(ready.at[1], 1))
    when(sends_back, start(back_copies(0)))

    half = HEADS // 2

    def opening(h, _):
        @pl.when(h == 2)
        def _():
            arrive(1, 1)
            pass_on(1, 1)

        wait_queries(h)

        @pl.when(h == 0)
        def _():
            pass_on(0, 0)

        unit(h, diag, fresh=True)
        return 0

    lax.fori_loop(0, half, opening, 0)
    arrive(1, 0)
    pass_on(1, 0)
    relay_back()

    @pl.when(z >= 1)
    def _():
        sweep(0, half, full(1))

    arrive(2, 1)
    pass_on(2, 1)

    def middle(h, _):
        wait_queries(h)

        @pl.when(h == half + 2)
        def _():
            arrive(2, 0)
            pass_on(2, 0)

        @pl.when(z >= 1)
        def _():
            unit(h, diag + full(1), fresh=True)

        @pl.when(z < 1)
        def _():
            unit(h, diag, fresh=True)

        return 0

    lax.fori_loop(half, HEADS, middle, 0)

    def relay(h):
        @pl.when(h == 1)
        def _():
            arrive(3, 1)
            pass_on(3, 1)

    @pl.when(z >= 2)
    def _():
        sweep(0, HEADS, full(2), before=relay)

    arrive(3, 0)

    @pl.when(z >= WINDOW)
    def _():
        wait_half(ring_recv.at[WINDOW - 1, 1])
        wait_half(back_recv.at[1])
        sweep(0, HEADS, full(3) + far, after=finish)

    @pl.when(z == 3)
    def _():
        sweep(0, HEADS, full(3), after=finish)

    @pl.when(z < 3)
    def _():
        def body(h, _):
            finish(h)
            return 0

        lax.fori_loop(0, HEADS, body, 0)

    others = GROUP - 1
    wait_bytes(kb.at[0, pl.ds(0, others * TOK), :], kv_send.at[0])
    wait_bytes(v_turned.at[pl.ds(0, others)], kv_send.at[1])
    wait_bytes(qb.at[pl.ds(0, others)], q_send.at[0])
    for s in range(WINDOW):
        for j in range(2):
            if (s, j) != (WINDOW - 1, 0):
                when((z >= s) & (z < slices - 1), lambda s=s, j=j: wait_half(ring_send.at[s, j]))
    when(sends_back, lambda: wait_half(back_send.at[0]))
    when(relays, lambda: wait_half(back_send.at[1]))
    wait_bytes(done.at[pl.ds(0, others)], out_send.at[0])
    wait_bytes(out, out_recv.at[0])


def solution(mesh):
    slices = mesh.shape["head"] // GROUP

    def local(query, key, value, lengths):
        rows, width = query.shape[1:]
        hbm = pl.BlockSpec(memory_space=pl.ANY)
        dma = pltpu.SemaphoreType.DMA
        attended = pl.pallas_call(
            functools.partial(kernel, slices),
            out_shape=jax.ShapeDtypeStruct((rows, width), BF16),
            in_specs=[pl.BlockSpec(memory_space=pltpu.SMEM), hbm, hbm, hbm],
            out_specs=hbm,
            scratch_shapes=[
                pltpu.VMEM((HEADS, SLICE, DIM), BF16),
                pltpu.VMEM((WINDOW + 1, SLICE, DIM), BF16),
                pltpu.VMEM((WINDOW + 1, DIM, SLICE), BF16),
                pltpu.VMEM((TOK, GROUP * DIM), BF16),
                pltpu.VMEM((GROUP, DIM, TOK), BF16),
                pltpu.VMEM((SLICE, DIM), BF16),
                pltpu.VMEM((WINDOW + 1, SLICE, DIM), BF16),
                pltpu.VMEM((HEADS, 1, SLICE), F32),
                pltpu.VMEM((HEADS, 1, SLICE), F32),
                pltpu.VMEM((HEADS, DIM, SLICE), F32),
                pltpu.VMEM((SLICE, QB), F32),
                pltpu.VMEM((1, QB), F32),
                pltpu.VMEM((HEADS, SLICE, DIM), BF16),
                pltpu.VMEM((HALF, DIM), BF16),
                pltpu.VMEM((DIM, HALF), BF16),
                dma((1,)),
                dma((HEADS,)),
                dma((2,)),
                dma((2,)),
                dma((WINDOW, 2)),
                dma((WINDOW, 2)),
                dma((2,)),
                dma((2,)),
                dma((1,)),
                dma((1,)),
                dma((1,)),
                pltpu.SemaphoreType.REGULAR((3,)),
            ],
            compiler_params=pltpu.CompilerParams(collective_id=0, has_side_effects=True, vmem_limit_bytes=56 * 2**20),
        )(lengths, query[0], key[0], value[0])
        return attended[None]

    placed = (P("rep", "head", None), P("rep", "head", None), P("rep", "head", None), P("rep", None))
    return jax.shard_map(local, mesh=mesh, in_specs=placed, out_specs=P("rep", "head", None), check_vma=False)
```

```python
import functools

import jax
import jax.numpy as jnp
from jax import lax
from jax.experimental import pallas as pl
from jax.experimental.pallas import tpu as pltpu
from jax.sharding import PartitionSpec as P

MESH = pl.DeviceIdType.MESH
F32 = jnp.float32
BF16 = jnp.bfloat16

HEADS = 8
DIM = 128
DOCS = 8
GROUP = 8
TOK = 128
SLICE = GROUP * TOK
HALF = SLICE // 2
BACK = SLICE * 3 // 4
MOST = 6
WINDOW = 4
QB = 512
EDGE = 256
LOG2E_SCALE = 1.4426950408889634 * DIM**-0.5
OFF = -1e30


def kernel(slices, lengths, q_in, k_in, v_in, out, qb, kb, vt, v_raw, v_turned, q_doc, k_doc,
           top, total, accum, held, held_top, done,
           k_relay, v_relay,
           q_send, q_recv, kv_send, kv_recv, ring_send, ring_recv, back_send, back_recv, out_send, out_recv, local_sem, ready):
    rep = lax.axis_index("rep")
    me = lax.axis_index("head")
    z, g = me // GROUP, me % GROUP

    def peer(t):
        return (g + t) % GROUP

    def device(zz, gg):
        return (rep, zz * GROUP + gg)

    def block(i, size=TOK):
        return pl.ds(pl.multiple_of(i * size, size), size)

    def when(condition, action):
        pl.when(condition)(action)

    barrier = pltpu.get_barrier_semaphore()

    def greet(zz):
        pl.semaphore_signal(barrier, inc=1, device_id=device(zz, g), device_id_type=MESH)

    def answer(i, zz):
        pl.semaphore_signal(ready.at[i], inc=1, device_id=device(zz, g), device_id_type=MESH)

    v_load = pltpu.make_async_copy(v_in, v_raw, local_sem.at[0])
    v_load.start()
    for t in range(1, GROUP):
        pl.semaphore_signal(barrier, inc=1, device_id=device(z, peer(t)), device_id_type=MESH)
    when(z < slices - 1, lambda: greet(z + 1))
    when(z == 0, lambda: greet(slices - 1))
    when(z == WINDOW, lambda: greet(slices - 1))
    when(z < slices - 1 - WINDOW, lambda: greet(z + 1 + WINDOW))
    expected = jnp.where(z > 0, GROUP, GROUP - 1) + jnp.where(z > WINDOW, 1, 0) + jnp.where(z == slices - 1, 2, 0)
    pl.semaphore_wait(barrier, expected)
    when(z > 0, lambda: answer(0, z - 1))
    when(z == slices - 1, lambda: answer(1, 0))
    when(z > WINDOW, lambda: answer(2, z - 1 - WINDOW))

    def copy_to(t, src, dst, send, recv):
        if t == 0:
            return pltpu.make_async_copy(src, dst, recv)
        return pltpu.make_async_remote_copy(src, dst, send, recv, device_id=device(z, peer(t)), device_id_type=MESH)

    def k_copy(t):
        return copy_to(t, k_in.at[:, block(peer(t))], kb.at[0, block(g), :], kv_send.at[0], kv_recv.at[0])

    def v_copy(t):
        return copy_to(t, v_turned.at[peer(t)], vt.at[0, :, block(g)], kv_send.at[1], kv_recv.at[1])

    def q_copy(h, t):
        return copy_to(t, q_in.at[:, block(peer(t) * HEADS + h)], qb.at[h, block(g), :], q_send.at[0], q_recv.at[h])

    def out_copy(h, t):
        return copy_to(t, done.at[h, block(peer(t)), :], out.at[:, block(g * HEADS + h)], out_send.at[0], out_recv.at[0])

    def wait_bytes(ref, sem):
        pltpu.make_async_copy(ref, ref, sem).wait()

    def part_refs(s, lo, hi):
        part = pl.ds(lo, hi - lo)
        return kb.at[s, part, :], vt.at[s, :, part]

    def remote(pairs, send, recv, to):
        return [pltpu.make_async_remote_copy(src, dst, send, recv, device_id=device(to, g), device_id_type=MESH) for src, dst in pairs]

    def ring_copies(s, j):
        lo, hi = (BACK, SLICE) if s == WINDOW - 1 else (j * HALF, (j + 1) * HALF)
        return remote(zip(part_refs(s, lo, hi), part_refs(s + 1, lo, hi)), ring_send.at[s, j], ring_recv.at[s, j], (z + 1) % slices)

    def back_copies(hop):
        if hop == 0:
            return remote(zip(part_refs(0, 0, BACK), (k_relay, v_relay)), back_send.at[0], back_recv.at[0], (z + slices - 1) % slices)
        return remote(zip((k_relay, v_relay), part_refs(WINDOW, 0, BACK)), back_send.at[1], back_recv.at[1], (z + WINDOW + 1) % slices)

    def wait_ring(sem, s):
        wait_bytes(kb.at[0, pl.ds(0, 2 * (SLICE - BACK)), :] if s == WINDOW - 1 else kb.at[0], sem)

    def wait_back(sem):
        wait_bytes(kb.at[pl.ds(0, 3), pl.ds(0, 2 * BACK // 3), :], sem)

    sends_back = z < slices - WINDOW
    relays = (z < slices - 1 - WINDOW) | (z == slices - 1)

    for t in range(GROUP):
        k_copy(t).start()
    v_load.wait()
    for i in range(GROUP):
        v_turned[i] = v_raw[:, i * TOK:(i + 1) * TOK].astype(F32).T.astype(BF16)
    for t in range(GROUP):
        v_copy(t).start()

    def send_queries(h, _):
        for t in range(GROUP):
            q_copy(h, t).start()
        return 0

    lax.fori_loop(0, HEADS, send_queries, 0)

    lane = lax.broadcasted_iota(jnp.int32, (1, DIM), 1)
    first = jnp.zeros((1, DIM), jnp.int32)
    last = jnp.zeros((1, DIM), jnp.int32)
    end = jnp.int32(0)
    for d in range(DOCS):
        begin = end
        end = end + lengths[0, d]
        first = jnp.where(lane == d, begin, first)
        last = jnp.where(lane == d, end, last)
    row = lax.broadcasted_iota(jnp.int32, (SLICE, DIM), 0)

    def within(base):
        spot = row + base
        return (spot >= first) & (spot < last)

    q_doc[...] = jnp.where(within(z * SLICE) | (lane >= DOCS), jnp.float32(0), jnp.float32(OFF)).astype(BF16)

    def fill(s, _):
        k_doc[s] = jnp.where(within((z - s) * SLICE), jnp.float32(1), jnp.float32(0)).astype(BF16)
        return 0

    lax.fori_loop(0, WINDOW + 1, fill, 0)

    def scores(h, step):
        q_lo, q_hi, s, lo, hi, diagonal = step
        query = jnp.concatenate([qb[h, q_lo:q_hi, :], q_doc[q_lo:q_hi, :]], axis=1)
        keys = jnp.concatenate([kb[s, lo:hi, :], k_doc[s, lo:hi, :]], axis=1)
        found = lax.dot_general(keys, query, (((1,), (1,)), ((), ())), preferred_element_type=F32)
        if diagonal:
            k_pos = lax.broadcasted_iota(jnp.int32, found.shape, 0) + lo
            q_pos = lax.broadcasted_iota(jnp.int32, found.shape, 1) + q_lo
            found = jnp.where(k_pos <= q_pos, found, jnp.float32(OFF))
        return found, jnp.max(found, axis=0, keepdims=True)

    def unit(h, steps, fresh=False, following=None):
        state = {}
        size = steps[0][4] - steps[0][3]
        now = (held[:size, :], held_top[...]) if following is not None else scores(h, steps[0])
        for i, (q_lo, q_hi, s, lo, hi, _) in enumerate(steps):
            edges = range(q_lo, q_hi, EDGE)
            later = None
            if i + 1 < len(steps):
                later = scores(h, steps[i + 1])
            elif following is not None:
                held[:size, :], held_top[...] = scores(following, steps[0])
            found, best = now
            for e in edges:
                if e not in state and not fresh:
                    cols = slice(e, e + EDGE)
                    state[e] = (top[h, :, cols], total[h, :, cols], accum[h, :, cols])
            known = edges[0] in state
            if known:
                old, norm, acc = (jnp.concatenate(parts, axis=1) for parts in zip(*(state[e] for e in edges)))
                best = jnp.maximum(old, best)
            weights = jnp.exp2((found - best) * LOG2E_SCALE)
            product = jnp.dot(vt[s, :, lo:hi], weights.astype(BF16), preferred_element_type=F32)
            added = jnp.sum(weights, axis=0, keepdims=True)
            if known:
                factor = jnp.exp2((old - best) * LOG2E_SCALE)
                added, product = norm * factor + added, acc * factor + product
            for e in edges:
                part = slice(e - q_lo, e - q_lo + EDGE)
                state[e] = (best[:, part], added[:, part], product[:, part])
                if not any(other[0] <= e < other[1] for other in steps[i + 1:]):
                    cols = slice(e, e + EDGE)
                    top[h, :, cols], total[h, :, cols], accum[h, :, cols] = state[e]
            now = later

    blocks = SLICE // QB
    diag, far = [], []
    for lo in range(0, SLICE, QB):
        diag += [(lo, lo + QB, 0, 0, lo + EDGE, True), (lo + EDGE, lo + QB, 0, lo + EDGE, lo + QB, True)]
        far += [(lo, lo + QB, WINDOW, lo + EDGE, SLICE, False), (lo, lo + EDGE, WINDOW, lo, lo + EDGE, False)]

    def full(s):
        return [(lo, lo + QB, s, 0, SLICE, False) for lo in range(0, SLICE, QB)]

    def sweep(lo, hi, steps, before=None, after=None):
        held[:steps[0][4] - steps[0][3], :], held_top[...] = scores(lo, steps[0])

        def body(h, _):
            if before is not None:
                before(h)
            unit(h, steps, following=jnp.minimum(h + 1, hi - 1))
            if after is not None:
                after(h)
            return 0

        lax.fori_loop(lo, hi, body, 0)

    def wait_queries(h):
        wait_bytes(qb.at[h], q_recv.at[h])

    def start(copies):
        def act():
            for copy in copies:
                copy.start()
        return act

    def arrive(s, j):
        when(z >= s, lambda: wait_ring(ring_recv.at[s - 1, j], s - 1))

    def pass_on(s, j):
        when((z >= s) & (z < slices - 1), start(ring_copies(s, j)))

    def relay_back():
        when(z < slices - 1 - WINDOW, lambda: pl.semaphore_wait(ready.at[2], 1))
        when(relays, lambda: wait_back(back_recv.at[0]))
        when(relays, start(back_copies(1)))

    def finish(h):
        for b in range(blocks):
            cols = slice(b * QB, (b + 1) * QB)
            done[h, cols, :] = (accum[h, :, cols] / total[h, :, cols]).T.astype(BF16)
        for t in range(GROUP):
            out_copy(h, t).start()

    wait_bytes(kb.at[0], kv_recv.at[0])
    wait_bytes(vt.at[0], kv_recv.at[1])
    when(z < slices - 1, lambda: pl.semaphore_wait(ready.at[0], 1))
    pass_on(0, 1)
    when(z == 0, lambda: pl.semaphore_wait(ready.at[1], 1))
    when(sends_back, start(back_copies(0)))

    half = HEADS // 2

    def opening(h, _):
        @pl.when(h == 2)
        def _():
            arrive(1, 1)
            pass_on(1, 1)

        when(h == half - 1, relay_back)
        wait_queries(h)

        @pl.when(h == 0)
        def _():
            pass_on(0, 0)

        unit(h, diag, fresh=True)
        return 0

    lax.fori_loop(0, half, opening, 0)
    arrive(1, 0)
    pass_on(1, 0)

    @pl.when(z >= 1)
    def _():
        sweep(0, half, full(1))

    arrive(2, 1)
    pass_on(2, 1)

    def middle(h, _):
        wait_queries(h)

        @pl.when(h == half + 2)
        def _():
            arrive(2, 0)
            pass_on(2, 0)

        @pl.when(z >= 1)
        def _():
            unit(h, diag + full(1), fresh=True)

        @pl.when(z < 1)
        def _():
            unit(h, diag, fresh=True)

        return 0

    lax.fori_loop(half, HEADS, middle, 0)

    def relay(h):
        @pl.when(h == 1)
        def _():
            arrive(3, 1)
            pass_on(3, 1)

    when(z >= 2, lambda: sweep(0, MOST, full(2), before=relay))
    arrive(3, 0)

    @pl.when(z >= WINDOW)
    def _():
        wait_back(back_recv.at[1])
        wait_ring(ring_recv.at[WINDOW - 1, 1], WINDOW - 1)
        sweep(0, MOST, full(3) + far, after=finish)
        sweep(MOST, HEADS, full(2) + full(3) + far, after=finish)

    @pl.when(z == 3)
    def _():
        sweep(0, MOST, full(3), after=finish)
        sweep(MOST, HEADS, full(2) + full(3), after=finish)

    @pl.when(z < 3)
    def _():
        when(z == 2, lambda: sweep(MOST, HEADS, full(2)))

        def body(h, _):
            finish(h)
            return 0

        lax.fori_loop(0, HEADS, body, 0)

    others = GROUP - 1
    wait_bytes(kb.at[0, pl.ds(0, others * TOK), :], kv_send.at[0])
    wait_bytes(v_turned.at[pl.ds(0, others)], kv_send.at[1])
    wait_bytes(qb.at[pl.ds(0, others)], q_send.at[0])
    for s in range(WINDOW):
        for j in range(2):
            if (s, j) != (WINDOW - 1, 0):
                when((z >= s) & (z < slices - 1), lambda s=s, j=j: wait_ring(ring_send.at[s, j], s))
    when(sends_back, lambda: wait_back(back_send.at[0]))
    when(relays, lambda: wait_back(back_send.at[1]))
    wait_bytes(done.at[pl.ds(0, others)], out_send.at[0])
    wait_bytes(out, out_recv.at[0])


def solution(mesh):
    slices = mesh.shape["head"] // GROUP

    def local(query, key, value, lengths):
        rows, width = query.shape[1:]
        hbm = pl.BlockSpec(memory_space=pl.ANY)
        dma = pltpu.SemaphoreType.DMA
        attended = pl.pallas_call(
            functools.partial(kernel, slices),
            out_shape=jax.ShapeDtypeStruct((rows, width), BF16),
            in_specs=[pl.BlockSpec(memory_space=pltpu.SMEM), hbm, hbm, hbm],
            out_specs=hbm,
            scratch_shapes=[
                pltpu.VMEM((HEADS, SLICE, DIM), BF16),
                pltpu.VMEM((WINDOW + 1, SLICE, DIM), BF16),
                pltpu.VMEM((WINDOW + 1, DIM, SLICE), BF16),
                pltpu.VMEM((TOK, GROUP * DIM), BF16),
                pltpu.VMEM((GROUP, DIM, TOK), BF16),
                pltpu.VMEM((SLICE, DIM), BF16),
                pltpu.VMEM((WINDOW + 1, SLICE, DIM), BF16),
                pltpu.VMEM((HEADS, 1, SLICE), F32),
                pltpu.VMEM((HEADS, 1, SLICE), F32),
                pltpu.VMEM((HEADS, DIM, SLICE), F32),
                pltpu.VMEM((SLICE, QB), F32),
                pltpu.VMEM((1, QB), F32),
                pltpu.VMEM((HEADS, SLICE, DIM), BF16),
                pltpu.VMEM((BACK, DIM), BF16),
                pltpu.VMEM((DIM, BACK), BF16),
                dma((1,)),
                dma((HEADS,)),
                dma((2,)),
                dma((2,)),
                dma((WINDOW, 2)),
                dma((WINDOW, 2)),
                dma((2,)),
                dma((2,)),
                dma((1,)),
                dma((1,)),
                dma((1,)),
                pltpu.SemaphoreType.REGULAR((3,)),
            ],
            compiler_params=pltpu.CompilerParams(collective_id=0, has_side_effects=True, vmem_limit_bytes=56 * 2**20),
        )(lengths, query[0], key[0], value[0])
        return attended[None]

    placed = (P("rep", "head", None), P("rep", "head", None), P("rep", "head", None), P("rep", None))
    return jax.shard_map(local, mesh=mesh, in_specs=placed, out_specs=P("rep", "head", None), check_vma=False)
```

```python
import functools

import jax
import jax.numpy as jnp
from jax import lax
from jax.experimental import pallas as pl
from jax.experimental.pallas import tpu as pltpu
from jax.sharding import PartitionSpec as P

MESH = pl.DeviceIdType.MESH
F32 = jnp.float32
BF16 = jnp.bfloat16

HEADS = 8
DIM = 128
DOCS = 8
GROUP = 8
TOK = 128
SLICE = GROUP * TOK
HALF = SLICE // 2
BACK = SLICE * 3 // 4
MOST = 6
WINDOW = 4
QB = 512
EDGE = 256
LOG2E_SCALE = 1.4426950408889634 * DIM**-0.5
OFF = -1e30
PIECES = 8


def kernel(slices, lengths, q_in, k_in, v_in, out, qb, kb, vt, v_raw, v_turned, q_doc, k_doc,
           top, total, accum, held, held_top, done,
           k_relay, v_relay,
           q_send, q_recv, kv_send, kv_recv, ring_send, ring_recv, back_send, back_recv, out_send, out_recv, local_sem, ready):
    rep = lax.axis_index("rep")
    me = lax.axis_index("head")
    z, g = me // GROUP, me % GROUP

    def peer(t):
        return (g + t) % GROUP

    def device(zz, gg):
        return (rep, zz * GROUP + gg)

    def block(i, size=TOK):
        return pl.ds(pl.multiple_of(i * size, size), size)

    def when(condition, action):
        pl.when(condition)(action)

    barrier = pltpu.get_barrier_semaphore()

    def greet(zz):
        pl.semaphore_signal(barrier, inc=1, device_id=device(zz, g), device_id_type=MESH)

    def answer(i, zz):
        pl.semaphore_signal(ready.at[i], inc=1, device_id=device(zz, g), device_id_type=MESH)

    v_load = pltpu.make_async_copy(v_in, v_raw, local_sem.at[0])
    v_load.start()
    for t in range(1, GROUP):
        pl.semaphore_signal(barrier, inc=1, device_id=device(z, peer(t)), device_id_type=MESH)
    when(z < slices - 1, lambda: greet(z + 1))
    when(z == 0, lambda: greet(slices - 1))
    when(z == WINDOW, lambda: greet(slices - 1))
    when(z < slices - 1 - WINDOW, lambda: greet(z + 1 + WINDOW))
    expected = jnp.where(z > 0, GROUP, GROUP - 1) + jnp.where(z > WINDOW, 1, 0) + jnp.where(z == slices - 1, 2, 0)
    pl.semaphore_wait(barrier, expected)
    when(z > 0, lambda: answer(0, z - 1))
    when(z == slices - 1, lambda: answer(1, 0))
    when(z > WINDOW, lambda: answer(2, z - 1 - WINDOW))

    def copy_to(t, src, dst, send, recv):
        if t == 0:
            return pltpu.make_async_copy(src, dst, recv)
        return pltpu.make_async_remote_copy(src, dst, send, recv, device_id=device(z, peer(t)), device_id_type=MESH)

    def k_copy(t):
        return copy_to(t, k_in.at[:, block(peer(t))], kb.at[0, block(g), :], kv_send.at[0], kv_recv.at[0])

    def v_copy(t):
        return copy_to(t, v_turned.at[peer(t)], vt.at[0, :, block(g)], kv_send.at[1], kv_recv.at[1])

    def q_copy(h, t):
        return copy_to(t, q_in.at[:, block(peer(t) * HEADS + h)], qb.at[h, block(g), :], q_send.at[0], q_recv.at[h])

    def out_copy(h, t):
        return copy_to(t, done.at[h, block(peer(t)), :], out.at[:, block(g * HEADS + h)], out_send.at[0], out_recv.at[0])

    def wait_bytes(ref, sem):
        pltpu.make_async_copy(ref, ref, sem).wait()

    def part_refs(s, lo, hi):
        part = pl.ds(lo, hi - lo)
        return kb.at[s, part, :], vt.at[s, :, part]

    def remote(pairs, send, recv, to):
        return [pltpu.make_async_remote_copy(src, dst, send, recv, device_id=device(to, g), device_id_type=MESH) for src, dst in pairs]

    def ring_copies(s, j):
        lo, hi = (BACK, SLICE) if s == WINDOW - 1 else (j * HALF, (j + 1) * HALF)
        return remote(zip(part_refs(s, lo, hi), part_refs(s + 1, lo, hi)), ring_send.at[s, j], ring_recv.at[s, j], (z + 1) % slices)

    def back_copies(hop):
        if hop == 0:
            return remote(zip(part_refs(0, 0, BACK), (k_relay, v_relay)), back_send.at[0], back_recv.at[0], (z + slices - 1) % slices)
        return remote(zip((k_relay, v_relay), part_refs(WINDOW, 0, BACK)), back_send.at[1], back_recv.at[1], (z + WINDOW + 1) % slices)

    def wait_ring(sem, s):
        wait_bytes(kb.at[0, pl.ds(0, 2 * (SLICE - BACK)), :] if s == WINDOW - 1 else kb.at[0], sem)

    def wait_back(sem):
        wait_bytes(kb.at[pl.ds(0, 3), pl.ds(0, 2 * BACK // 3), :], sem)

    sends_back = z < slices - WINDOW
    relays = (z < slices - 1 - WINDOW) | (z == slices - 1)

    for t in range(GROUP):
        k_copy(t).start()
    v_load.wait()
    for i in range(GROUP):
        v_turned[i] = v_raw[:, i * TOK:(i + 1) * TOK].astype(F32).T.astype(BF16)
    for t in range(GROUP):
        v_copy(t).start()

    def send_queries(h, _):
        for t in range(GROUP):
            q_copy(h, t).start()
        return 0

    lax.fori_loop(0, HEADS, send_queries, 0)

    lane = lax.broadcasted_iota(jnp.int32, (1, DIM), 1)
    first = jnp.zeros((1, DIM), jnp.int32)
    last = jnp.zeros((1, DIM), jnp.int32)
    end = jnp.int32(0)
    for d in range(DOCS):
        begin = end
        end = end + lengths[0, d]
        first = jnp.where(lane == d, begin, first)
        last = jnp.where(lane == d, end, last)
    row = lax.broadcasted_iota(jnp.int32, (SLICE, DIM), 0)

    def within(base):
        spot = row + base
        return (spot >= first) & (spot < last)

    q_doc[...] = jnp.where(within(z * SLICE) | (lane >= DOCS), jnp.float32(0), jnp.float32(OFF)).astype(BF16)

    def fill(s, _):
        k_doc[s] = jnp.where(within((z - s) * SLICE), jnp.float32(1), jnp.float32(0)).astype(BF16)
        return 0

    lax.fori_loop(0, WINDOW + 1, fill, 0)

    def scores(h, step):
        q_lo, q_hi, s, lo, hi, diagonal = step
        query = jnp.concatenate([qb[h, q_lo:q_hi, :], q_doc[q_lo:q_hi, :]], axis=1)
        keys = jnp.concatenate([kb[s, lo:hi, :], k_doc[s, lo:hi, :]], axis=1)
        found = lax.dot_general(keys, query, (((1,), (1,)), ((), ())), preferred_element_type=F32)
        if diagonal:
            k_pos = lax.broadcasted_iota(jnp.int32, found.shape, 0) + lo
            q_pos = lax.broadcasted_iota(jnp.int32, found.shape, 1) + q_lo
            found = jnp.where(k_pos <= q_pos, found, jnp.float32(OFF))
        return found, jnp.max(found, axis=0, keepdims=True)

    def unit(h, steps, fresh=False, following=None):
        state = {}
        size = steps[0][4] - steps[0][3]
        now = (held[:size, :], held_top[...]) if following is not None else scores(h, steps[0])
        for i, (q_lo, q_hi, s, lo, hi, _) in enumerate(steps):
            edges = range(q_lo, q_hi, EDGE)
            later = None
            if i + 1 < len(steps):
                later = scores(h, steps[i + 1])
            elif following is not None:
                held[:size, :], held_top[...] = scores(following, steps[0])
            found, best = now
            for e in edges:
                if e not in state and not fresh:
                    cols = slice(e, e + EDGE)
                    state[e] = (top[h, :, cols], total[h, :, cols], accum[h, :, cols])
            known = edges[0] in state
            if known:
                old, norm, acc = (jnp.concatenate(parts, axis=1) for parts in zip(*(state[e] for e in edges)))
                best = jnp.maximum(old, best)
            weights = jnp.exp2((found - best) * LOG2E_SCALE)
            product = jnp.dot(vt[s, :, lo:hi], weights.astype(BF16), preferred_element_type=F32)
            added = jnp.sum(weights, axis=0, keepdims=True)
            if known:
                factor = jnp.exp2((old - best) * LOG2E_SCALE)
                added, product = norm * factor + added, acc * factor + product
            for e in edges:
                part = slice(e - q_lo, e - q_lo + EDGE)
                state[e] = (best[:, part], added[:, part], product[:, part])
                if not any(other[0] <= e < other[1] for other in steps[i + 1:]):
                    cols = slice(e, e + EDGE)
                    top[h, :, cols], total[h, :, cols], accum[h, :, cols] = state[e]
            now = later

    blocks = SLICE // QB
    diag, far = [], []
    for lo in range(0, SLICE, QB):
        diag += [(lo, lo + QB, 0, 0, lo + EDGE, True), (lo + EDGE, lo + QB, 0, lo + EDGE, lo + QB, True)]
        far += [(lo, lo + QB, WINDOW, lo + EDGE, SLICE, False), (lo, lo + EDGE, WINDOW, lo, lo + EDGE, False)]

    def full(s):
        return [(lo, lo + QB, s, 0, SLICE, False) for lo in range(0, SLICE, QB)]

    def sweep(lo, hi, steps, before=None, after=None):
        held[:steps[0][4] - steps[0][3], :], held_top[...] = scores(lo, steps[0])

        def body(h, _):
            if before is not None:
                before(h)
            unit(h, steps, following=jnp.minimum(h + 1, hi - 1))
            if after is not None:
                after(h)
            return 0

        lax.fori_loop(lo, hi, body, 0)

    def wait_queries(h):
        wait_bytes(qb.at[h], q_recv.at[h])

    def start(copies):
        def act():
            for copy in copies:
                copy.start()
        return act

    def arrive(s, j):
        when(z >= s, lambda: wait_ring(ring_recv.at[s - 1, j], s - 1))

    def pass_on(s, j):
        when((z >= s) & (z < slices - 1), start(ring_copies(s, j)))

    def relay_back():
        when(z < slices - 1 - WINDOW, lambda: pl.semaphore_wait(ready.at[2], 1))
        when(relays, lambda: wait_back(back_recv.at[0]))
        when(relays, start(back_copies(1)))

    def finish(h):
        for b in range(blocks):
            cols = slice(b * QB, (b + 1) * QB)
            done[h, cols, :] = (accum[h, :, cols] / total[h, :, cols]).T.astype(BF16)
        for t in range(GROUP):
            out_copy(h, t).start()

    wait_bytes(kb.at[0], kv_recv.at[0])
    wait_bytes(vt.at[0], kv_recv.at[1])
    when(z < slices - 1, lambda: pl.semaphore_wait(ready.at[0], 1))
    pass_on(0, 1)
    when(z == 0, lambda: pl.semaphore_wait(ready.at[1], 1))
    when(sends_back, start(back_copies(0)))

    half = HEADS // 2

    def opening(h, _):
        @pl.when(h == 2)
        def _():
            arrive(1, 1)
            pass_on(1, 1)

        when(h == half - 1, relay_back)
        wait_queries(h)

        @pl.when(h == 0)
        def _():
            pass_on(0, 0)

        unit(h, diag, fresh=True)
        return 0

    lax.fori_loop(0, half, opening, 0)
    arrive(1, 0)
    pass_on(1, 0)

    @pl.when(z >= 1)
    def _():
        sweep(0, half, full(1))

    arrive(2, 1)
    pass_on(2, 1)

    def middle(h, _):
        wait_queries(h)

        @pl.when(h == half + 2)
        def _():
            arrive(2, 0)
            pass_on(2, 0)

        @pl.when(z >= 1)
        def _():
            unit(h, diag + full(1), fresh=True)

        @pl.when(z < 1)
        def _():
            unit(h, diag, fresh=True)

        return 0

    lax.fori_loop(half, HEADS, middle, 0)

    def relay(h):
        @pl.when(h == 1)
        def _():
            arrive(3, 1)
            pass_on(3, 1)

    when(z >= 2, lambda: sweep(0, MOST, full(2), before=relay))
    arrive(3, 0)

    @pl.when(z >= WINDOW)
    def _():
        wait_back(back_recv.at[1])
        wait_ring(ring_recv.at[WINDOW - 1, 1], WINDOW - 1)
        sweep(0, MOST, full(3) + far, after=finish)
        sweep(MOST, HEADS, full(2) + full(3) + far, after=finish)

    @pl.when(z == 3)
    def _():
        sweep(0, MOST, full(3), after=finish)
        sweep(MOST, HEADS, full(2) + full(3), after=finish)

    @pl.when(z < 3)
    def _():
        when(z == 2, lambda: sweep(MOST, HEADS, full(2)))

        def body(h, _):
            finish(h)
            return 0

        lax.fori_loop(0, HEADS, body, 0)

    others = GROUP - 1
    wait_bytes(kb.at[0, pl.ds(0, others * TOK), :], kv_send.at[0])
    wait_bytes(v_turned.at[pl.ds(0, others)], kv_send.at[1])
    wait_bytes(qb.at[pl.ds(0, others)], q_send.at[0])
    for s in range(WINDOW):
        for j in range(2):
            if (s, j) != (WINDOW - 1, 0):
                when((z >= s) & (z < slices - 1), lambda s=s, j=j: wait_ring(ring_send.at[s, j], s))
    when(sends_back, lambda: wait_back(back_send.at[0]))
    when(relays, lambda: wait_back(back_send.at[1]))
    wait_bytes(done.at[pl.ds(0, others)], out_send.at[0])
    wait_bytes(out, out_recv.at[0])


def place(src, dst, held, load_sem, store_sem):
    def copies(i):
        rows = pl.ds(i * (TOK // PIECES), TOK // PIECES)
        load = pltpu.make_async_copy(src.at[rows, :], held.at[rows, :], load_sem.at[i])
        return load, pltpu.make_async_copy(held.at[rows, :], dst.at[rows, :], store_sem.at[i])

    for i in range(PIECES):
        copies(i)[0].start()
    for i in range(PIECES):
        load, store = copies(i)
        load.wait()
        store.start()
    for i in range(PIECES):
        copies(i)[1].wait()


def solution(mesh):
    slices = mesh.shape["head"] // GROUP

    def local(query, key, value, lengths):
        rows, width = query.shape[1:]
        hbm = pl.BlockSpec(memory_space=pl.ANY)
        dma = pltpu.SemaphoreType.DMA
        attended = pl.pallas_call(
            functools.partial(kernel, slices),
            out_shape=jax.ShapeDtypeStruct((rows, width), BF16),
            in_specs=[pl.BlockSpec(memory_space=pltpu.SMEM), hbm, hbm, hbm],
            out_specs=hbm,
            scratch_shapes=[
                pltpu.VMEM((HEADS, SLICE, DIM), BF16),
                pltpu.VMEM((WINDOW + 1, SLICE, DIM), BF16),
                pltpu.VMEM((WINDOW + 1, DIM, SLICE), BF16),
                pltpu.VMEM((TOK, GROUP * DIM), BF16),
                pltpu.VMEM((GROUP, DIM, TOK), BF16),
                pltpu.VMEM((SLICE, DIM), BF16),
                pltpu.VMEM((WINDOW + 1, SLICE, DIM), BF16),
                pltpu.VMEM((HEADS, 1, SLICE), F32),
                pltpu.VMEM((HEADS, 1, SLICE), F32),
                pltpu.VMEM((HEADS, DIM, SLICE), F32),
                pltpu.VMEM((SLICE, QB), F32),
                pltpu.VMEM((1, QB), F32),
                pltpu.VMEM((HEADS, SLICE, DIM), BF16),
                pltpu.VMEM((BACK, DIM), BF16),
                pltpu.VMEM((DIM, BACK), BF16),
                dma((1,)),
                dma((HEADS,)),
                dma((2,)),
                dma((2,)),
                dma((WINDOW, 2)),
                dma((WINDOW, 2)),
                dma((2,)),
                dma((2,)),
                dma((1,)),
                dma((1,)),
                dma((1,)),
                pltpu.SemaphoreType.REGULAR((3,)),
            ],
            compiler_params=pltpu.CompilerParams(collective_id=0, has_side_effects=True, vmem_limit_bytes=56 * 2**20),
        )(lengths, query[0], key[0], value[0])
        return pl.pallas_call(
            place,
            out_shape=jax.ShapeDtypeStruct((rows, width), BF16),
            in_specs=[hbm],
            out_specs=hbm,
            scratch_shapes=[pltpu.VMEM((rows, width), BF16), dma((PIECES,)), dma((PIECES,))],
            compiler_params=pltpu.CompilerParams(vmem_limit_bytes=56 * 2**20),
        )(attended)[None]

    placed = (P("rep", "head", None), P("rep", "head", None), P("rep", "head", None), P("rep", None))
    return jax.shard_map(local, mesh=mesh, in_specs=placed, out_specs=P("rep", "head", None), check_vma=False)
```
